1024 devices in a mesh: replica: 64 (over z, y_hi, core), tensor: 16 (over y_lo, x).
Axes of the slice: x: 4, y: 8 (y_hi: 2, y_lo: 4; y = y_hi * 4 + y_lo), z: 16, core: 2. Of those that a mesh axis runs over, the one named last changes fastest.
Arguments:
- queries: bfloat16 [4096, 8192], P(('replica', 'tensor')), may hold values from -64 to 64
- stored_keys: bfloat16 [4096, 8, 128, 128], P(('replica', 'tensor')), may hold values from -4 to 4
- stored_values: bfloat16 [4096, 8, 128, 128], P(('replica', 'tensor')), may hold values from -6 to 6
- lengths: int32 [4096], P(('replica', 'tensor')), may hold values from 1 to 128
- hidden: bfloat16 [4096, 5120], P(('replica', 'tensor')), may hold values from -3 to 3
- output_weight: bfloat16 [8192, 5120], P('tensor'), may hold values from -0.0625 to 0.0625
- adapter_down: bfloat16 [128, 8192], P('replica', 'tensor'), may hold values from -0.0625 to 0.0625
- adapter_up: bfloat16 [128, 5120], P('replica', 'tensor'), may hold values from -0.5 to 0.5
Outputs:
- block_out: bfloat16 [4096, 5120], P(('replica', 'tensor'))
The draws below stay inside these ranges and needn't reach their ends.
All inputs are finite; a program needn't handle non-finite values.
Results may differ from the reference program's by a relative error of at most 0.007.
Values may be sent and summed in bfloat16 or wider, within the bound.
No kernel may reach another device: no remote copies, remote signals or barrier semaphores. Data moves between devices by JAX's collectives and lax.ppermute only.
A program may use at most 32 MiB of HBM per device.

```python
import math
import jax
import jax.numpy as jnp
from jax import lax

MODEL_WIDTH = 5120
QUERY_HEADS = 64
KVH = 8
HEAD_SIZE = 128
ADAPTER_RANK = 128
CACHE = 128
ROW_DEV = 4
GROUP = 8
ROWS = 4096
N_TENSOR = 16


def draw_stored_keys(key, part):
    key = jax.random.fold_in(key, 11)
    values = jax.random.truncated_normal(key, -3.9, 3.9, (ROWS, KVH, CACHE, HEAD_SIZE), jnp.float32)
    return values.astype(jnp.bfloat16)


def draw_queries(key, part):
    key = jax.random.fold_in(key, 5)
    values = jax.random.normal(key, (ROWS, QUERY_HEADS * HEAD_SIZE), jnp.float32)
    return values.astype(jnp.bfloat16)


def draw_lengths(key, part):
    key = jax.random.fold_in(key, 3)
    drawn = jax.random.randint(key, (ROWS,), 1, CACHE + 1, dtype=jnp.int32)
    index = jnp.arange(ROWS, dtype=jnp.int32)
    return jnp.where(index % 7 == 0, CACHE, drawn).astype(jnp.int32)


def block_levels(stream_key, shape, pieces, least, largest):
    loudness = 1.0
    for position, shards_of in pieces:
        steps = jax.random.uniform(jax.random.fold_in(jax.random.fold_in(stream_key, 6), position), (shards_of,), jnp.float32, least / len(pieces), largest / len(pieces))
        loudness = loudness * jnp.repeat(jnp.exp(steps), shape[position] // shards_of).reshape((-1,) + (1,) * (len(shape) - 1 - position))
    return loudness


def centred(own_key, dims, scale, limit, pieces=(), kind=jnp.bfloat16):
    factor_of = block_levels(own_key, dims, pieces, -0.22, 0.18) if pieces else 1.0
    values = jax.random.normal(own_key, dims, jnp.float32) * scale * factor_of
    return jnp.minimum(jnp.maximum(values, -limit), limit).astype(kind)


def setup_inputs(seed: int = 0) -> dict:
    seeds = jax.random.split(jax.random.key(seed), 9)
    queries = draw_queries(jax.random.fold_in(seeds[8], 71), 0)
    stored_keys = draw_stored_keys(jax.random.fold_in(seeds[8], 71), 0)
    stored_values = centred(seeds[2], (ROWS, KVH, CACHE, HEAD_SIZE), 1.0, 6.0, ((0, 1024),))
    lengths = draw_lengths(jax.random.fold_in(seeds[8], 71), 0)
    hidden = centred(seeds[4], (ROWS, MODEL_WIDTH), 0.5, 3.0, ((0, 1024),))
    output_weight = centred(seeds[5], (QUERY_HEADS * HEAD_SIZE, MODEL_WIDTH), (QUERY_HEADS * HEAD_SIZE) ** -0.5, 0.0625, ((0, 16),))
    adapter_down = centred(seeds[6], (ADAPTER_RANK, QUERY_HEADS * HEAD_SIZE), (QUERY_HEADS * HEAD_SIZE) ** -0.5, 0.0625, ((0, 64), (1, 16)))
    adapter_up = centred(seeds[7], (ADAPTER_RANK, MODEL_WIDTH), ADAPTER_RANK ** -0.5, 0.5, ((0, 64), (1, 16)))
    return dict(queries=queries, stored_keys=stored_keys, stored_values=stored_values, lengths=lengths, hidden=hidden, output_weight=output_weight, adapter_down=adapter_down, adapter_up=adapter_up)


adapter_scale = 2.0

def attend_block(query_block, key_block, value_block, length_block):
    count = query_block.shape[0]
    shaped = query_block.astype(jnp.float32).reshape(count, KVH, GROUP, HEAD_SIZE)
    scores = jnp.einsum('rkgd,rksd->rkgs', shaped, key_block.astype(jnp.float32)) / math.sqrt(HEAD_SIZE)
    positions = jnp.arange(CACHE, dtype=jnp.int32)
    visible = positions[None, :] < length_block[:, None]
    scores = jnp.where(visible[:, None, None, :], scores, -1e+30)
    highest = lax.optimization_barrier(jnp.max(scores, axis=-1, keepdims=True))
    expo = jnp.exp(scores - highest)
    denominator = lax.optimization_barrier(jnp.sum(expo, axis=-1, keepdims=True))
    probs = (expo / denominator).astype(jnp.bfloat16)
    attended = jnp.einsum('rkgs,rksd->rkgd', probs.astype(jnp.float32), value_block.astype(jnp.float32))
    return attended.astype(jnp.bfloat16).reshape(count, QUERY_HEADS * HEAD_SIZE)

def reference(queries, stored_keys, stored_values, lengths, hidden, output_weight, adapter_down, adapter_up):
    block_rows = ROW_DEV * N_TENSOR
    blocks = ROWS // block_rows
    stacked = (queries.reshape(blocks, block_rows, QUERY_HEADS * HEAD_SIZE), stored_keys.reshape(blocks, block_rows, KVH, CACHE, HEAD_SIZE), stored_values.reshape(blocks, block_rows, KVH, CACHE, HEAD_SIZE), lengths.reshape(blocks, block_rows))
    attended = lax.map(lambda items: attend_block(items[0], items[1], items[2], items[3]), stacked)
    attended = attended.reshape(ROWS, QUERY_HEADS * HEAD_SIZE)
    weight_delta = jnp.dot(adapter_down.T, adapter_up, preferred_element_type=jnp.float32)
    merged_weight = (output_weight.astype(jnp.float32) + adapter_scale * weight_delta).astype(jnp.bfloat16)
    projected = jnp.dot(attended, merged_weight, preferred_element_type=jnp.float32)
    return (hidden.astype(jnp.float32) + projected).astype(jnp.bfloat16)
```

```python
import math

import jax
import jax.numpy as jnp
from jax import lax
from jax.sharding import PartitionSpec as P

QUERY_HEADS = 64
KVH = 8
HEAD_SIZE = 128
CACHE = 128
GROUP = 8
N_TENSOR = 16
N_REPLICA = 64
INNER = 8

adapter_scale = 2.0

INNER_GROUPS = [[o * INNER + i for i in range(INNER)] for o in range(N_REPLICA // INNER)]
OUTER_GROUPS = [[o * INNER + i for o in range(N_REPLICA // INNER)] for i in range(INNER)]


def attend_rows(queries, stored_keys, stored_values, lengths):
    row_count = queries.shape[0]
    shaped = queries.reshape(row_count, KVH, GROUP, HEAD_SIZE)
    scores = jnp.einsum(
        "rkgd,rksd->rkgs", shaped, stored_keys, preferred_element_type=jnp.float32
    ) / math.sqrt(HEAD_SIZE)
    positions = jnp.arange(CACHE, dtype=jnp.int32)
    visible = positions[None, :] < lengths[:, None]
    scores = jnp.where(visible[:, None, None, :], scores, -1e30)
    highest = jnp.max(scores, axis=-1, keepdims=True)
    expo = jnp.exp(scores - highest)
    denominator = jnp.sum(expo, axis=-1, keepdims=True)
    probs = (expo / denominator).astype(jnp.bfloat16)
    attended = jnp.einsum(
        "rkgs,rksd->rkgd", probs, stored_values, preferred_element_type=jnp.float32
    )
    return attended.astype(jnp.bfloat16).reshape(row_count, QUERY_HEADS * HEAD_SIZE)


def spread(block, axis, groups=None):
    count = len(groups[0]) if groups else N_TENSOR
    copies = jnp.broadcast_to(block[None], (count,) + block.shape)
    return lax.all_to_all(copies, axis, 0, 0, axis_index_groups=groups)


def gather_adapter(adapter_down, adapter_up):
    both = jnp.concatenate([adapter_down, adapter_up], axis=1)
    rank, width = both.shape
    some = spread(both, "replica", INNER_GROUPS).reshape(INNER * rank, width)
    every = spread(some, "replica", OUTER_GROUPS).reshape(N_REPLICA * rank, width)
    return every[:, : adapter_down.shape[1]], every[:, adapter_down.shape[1] :]


def per_device(
    queries, stored_keys, stored_values, lengths, hidden, output_weight, adapter_down, adapter_up
):
    rows, width = hidden.shape
    down, up = gather_adapter(adapter_down, adapter_up)
    attended = attend_rows(queries, stored_keys, stored_values, lengths)
    blocks = attended.reshape(rows, N_TENSOR, -1).transpose(1, 0, 2)
    grouped = lax.all_to_all(blocks, "tensor", 0, 0).reshape(N_TENSOR * rows, -1)
    low_part = lax.dot_general(
        grouped, down, (((1,), (1,)), ((), ())), preferred_element_type=jnp.float32
    ).astype(jnp.bfloat16)
    low_parts = spread(low_part, "tensor")
    partial_value = jnp.dot(grouped, output_weight, preferred_element_type=jnp.float32)
    partial_value = partial_value.astype(jnp.bfloat16).reshape(N_TENSOR, rows, width)
    partials = lax.all_to_all(partial_value, "tensor", 0, 0)
    low = jnp.sum(low_parts.astype(jnp.float32), axis=0).astype(jnp.bfloat16)
    delta = adapter_scale * jnp.dot(low, up, preferred_element_type=jnp.float32)
    delta = lax.all_to_all(
        delta.astype(jnp.bfloat16).reshape(N_TENSOR, rows, -1), "tensor", 0, 0
    )
    delta = delta.transpose(1, 0, 2).reshape(rows, width).astype(jnp.float32)
    reduced = jnp.sum(partials.astype(jnp.float32), axis=0) + delta
    return (hidden.astype(jnp.float32) + reduced).astype(jnp.bfloat16)


def solution(mesh):
    in_specs = (
        P(("replica", "tensor"), None),
        P(("replica", "tensor"), None, None, None),
        P(("replica", "tensor"), None, None, None),
        P(("replica", "tensor")),
        P(("replica", "tensor"), None),
        P("tensor", None),
        P("replica", "tensor"),
        P("replica", "tensor"),
    )
    out_specs = P(("replica", "tensor"), None)
    return jax.shard_map(
        per_device, mesh=mesh, in_specs=in_specs, out_specs=out_specs, check_vma=False
    )
```

```python
import math

import jax
import jax.numpy as jnp
from jax import lax
from jax.sharding import PartitionSpec as P

QUERY_HEADS = 64
KVH = 8
HEAD_SIZE = 128
CACHE = 128
GROUP = 8
N_TENSOR = 16
N_REPLICA = 64
SIDE = 4

adapter_scale = 2.0

X_GROUPS = [[y * SIDE + x for x in range(SIDE)] for y in range(SIDE)]
Y_GROUPS = [[y * SIDE + x for y in range(SIDE)] for x in range(SIDE)]
FAR = 16
FAR_GROUPS = [
    [(2 * zz + odd) * 4 + hi * 2 + core for zz in range(8) for hi in range(2)]
    for odd in range(2)
    for core in range(2)
]


def attend_rows(queries, stored_keys, stored_values, lengths):
    row_count = queries.shape[0]
    shaped = queries.reshape(row_count, KVH, GROUP, HEAD_SIZE)
    scores = jnp.einsum(
        "rkgd,rksd->rkgs", shaped, stored_keys, preferred_element_type=jnp.float32
    ) / math.sqrt(HEAD_SIZE)
    positions = jnp.arange(CACHE, dtype=jnp.int32)
    visible = positions[None, :] < lengths[:, None]
    scores = jnp.where(visible[:, None, None, :], scores, -1e30)
    highest = jnp.max(scores, axis=-1, keepdims=True)
    expo = jnp.exp(scores - highest)
    denominator = jnp.sum(expo, axis=-1, keepdims=True)
    probs = (expo / denominator).astype(jnp.bfloat16)
    attended = jnp.einsum(
        "rkgs,rksd->rkgd", probs, stored_values, preferred_element_type=jnp.float32
    )
    return attended.astype(jnp.bfloat16).reshape(row_count, QUERY_HEADS * HEAD_SIZE)


def spread(block, axis, groups):
    copies = jnp.broadcast_to(block[None], (len(groups[0]),) + block.shape)
    return lax.all_to_all(copies, axis, 0, 0, axis_index_groups=groups)


def swap(block, axis, count, bit):
    return lax.ppermute(block, axis, [(i, i ^ bit) for i in range(count)])


def ordered(mine, other, upper):
    return jnp.where(upper, other, mine), jnp.where(upper, mine, other)


def gather_far(adapter_down, adapter_up):
    both = jnp.concatenate([adapter_down, adapter_up], axis=1)
    rank, width = both.shape
    return spread(both, "replica", FAR_GROUPS).reshape(FAR * rank, width)


def gather_near(some, split):
    for bit in (4, 1):
        other = swap(some, "replica", N_REPLICA, bit)
        some = jnp.concatenate([some, other], axis=0)
    return some[:, :split], some[:, split:]


def per_device(
    queries, stored_keys, stored_values, lengths, hidden, output_weight, adapter_down, adapter_up
):
    rows, width = hidden.shape
    quarter = width // SIDE
    tensor = lax.axis_index("tensor")
    some = gather_far(adapter_down, adapter_up)
    attended = attend_rows(queries, stored_keys, stored_values, lengths)
    blocks = attended.reshape(rows, N_TENSOR, -1).transpose(1, 0, 2)
    some, blocks = lax.optimization_barrier((some, blocks))
    down, up = gather_near(some, adapter_down.shape[1])
    ranks = down.shape[0]
    grouped = lax.all_to_all(blocks, "tensor", 0, 0)
    grouped = grouped.reshape(SIDE, SIDE, rows, -1).transpose(1, 0, 2, 3)
    grouped = grouped.reshape(N_TENSOR * rows, -1)

    other = swap(up, "tensor", N_TENSOR, 1)
    low_half, high_half = ordered(up, other, (tensor & 1) == 1)
    half = jnp.concatenate([low_half, high_half], axis=1)
    other = swap(half, "tensor", N_TENSOR, 2)
    low_half, high_half = ordered(half, other, (tensor & 2) == 2)
    up_quarter = jnp.concatenate([low_half, high_half], axis=1)

    partial_value = jnp.dot(grouped, output_weight, preferred_element_type=jnp.float32)
    low_part = lax.dot_general(
        grouped, down, (((1,), (1,)), ((), ())), preferred_element_type=jnp.float32
    )
    sent = jnp.concatenate(
        [partial_value.astype(jnp.bfloat16), low_part.astype(jnp.bfloat16)], axis=1
    ).reshape(SIDE, SIDE * rows, width + ranks)
    along_x = lax.all_to_all(sent, "tensor", 0, 0, axis_index_groups=X_GROUPS)

    low = jnp.sum(along_x[:, :, width:].astype(jnp.float32), axis=0).astype(jnp.bfloat16)
    low = spread(low, "tensor", Y_GROUPS)
    low = jnp.sum(low.astype(jnp.float32), axis=0).astype(jnp.bfloat16)
    delta = adapter_scale * jnp.dot(low, up_quarter, preferred_element_type=jnp.float32)
    summed = jnp.sum(along_x[:, :, :width].astype(jnp.float32), axis=0)
    column = lax.broadcasted_iota(jnp.int32, (1, width), 1)
    start = (tensor // SIDE) * quarter
    mine = (column >= start) & (column < start + quarter)
    summed = summed + jnp.where(mine, jnp.concatenate([delta] * SIDE, axis=1), 0.0)
    along_y = lax.all_to_all(
        summed.astype(jnp.bfloat16).reshape(SIDE, rows, width),
        "tensor",
        0,
        0,
        axis_index_groups=Y_GROUPS,
    )
    reduced = jnp.sum(along_y.astype(jnp.float32), axis=0)
    return (hidden.astype(jnp.float32) + reduced).astype(jnp.bfloat16)


def solution(mesh):
    in_specs = (
        P(("replica", "tensor"), None),
        P(("replica", "tensor"), None, None, None),
        P(("replica", "tensor"), None, None, None),
        P(("replica", "tensor")),
        P(("replica", "tensor"), None),
        P("tensor", None),
        P("replica", "tensor"),
        P("replica", "tensor"),
    )
    out_specs = P(("replica", "tensor"), None)
    return jax.shard_map(
        per_device, mesh=mesh, in_specs=in_specs, out_specs=out_specs, check_vma=False
    )
```

```python
import math

import jax
import jax.numpy as jnp
from jax import lax
from jax.sharding import PartitionSpec as P

QUERY_HEADS = 64
KVH = 8
HEAD_SIZE = 128
CACHE = 128
GROUP = 8
N_TENSOR = 16
N_REPLICA = 64

adapter_scale = 2.0

DEPTH = 16
Z_GROUPS = [[z * 4 + rest for z in range(DEPTH)] for rest in range(4)]


def attend_rows(queries, stored_keys, stored_values, lengths):
    row_count = queries.shape[0]
    shaped = queries.reshape(row_count, KVH, GROUP, HEAD_SIZE)
    scores = jnp.einsum(
        "rkgd,rksd->rkgs", shaped, stored_keys, preferred_element_type=jnp.float32
    ) / math.sqrt(HEAD_SIZE)
    positions = jnp.arange(CACHE, dtype=jnp.int32)
    visible = positions[None, :] < lengths[:, None]
    scores = jnp.where(visible[:, None, None, :], scores, -1e30)
    highest = jnp.max(scores, axis=-1, keepdims=True)
    expo = jnp.exp(scores - highest)
    denominator = jnp.sum(expo, axis=-1, keepdims=True)
    probs = (expo / denominator).astype(jnp.bfloat16)
    attended = jnp.einsum(
        "rkgs,rksd->rkgd", probs, stored_values, preferred_element_type=jnp.float32
    )
    return attended.astype(jnp.bfloat16).reshape(row_count, QUERY_HEADS * HEAD_SIZE)


def spread(block, axis, count, groups=None):
    copies = jnp.broadcast_to(block[None], (count,) + block.shape)
    return lax.all_to_all(copies, axis, 0, 0, axis_index_groups=groups)


def swap(block, axis, count, bit):
    return lax.ppermute(block, axis, [(i, i ^ bit) for i in range(count)])


def gather_along_z(adapter_down, adapter_up):
    both = jnp.concatenate([adapter_down, adapter_up], axis=1)
    rank, width = both.shape
    return spread(both, "replica", DEPTH, Z_GROUPS).reshape(DEPTH * rank, width)


def gather_rest(some, split):
    for bit in (2, 1):
        other = swap(some, "replica", N_REPLICA, bit)
        some = jnp.concatenate([some, other], axis=0)
    return some[:, :split], some[:, split:]


def per_device(
    queries, stored_keys, stored_values, lengths, hidden, output_weight, adapter_down, adapter_up
):
    rows, width = hidden.shape
    some = gather_along_z(adapter_down, adapter_up)
    attended = attend_rows(queries, stored_keys, stored_values, lengths)
    blocks = attended.reshape(rows, N_TENSOR, -1).transpose(1, 0, 2)
    some, blocks = lax.optimization_barrier((some, blocks))
    down, up = gather_rest(some, adapter_down.shape[1])
    grouped = lax.all_to_all(blocks, "tensor", 0, 0).reshape(N_TENSOR * rows, -1)

    low_part = lax.dot_general(
        grouped, down, (((1,), (1,)), ((), ())), preferred_element_type=jnp.float32
    ).astype(jnp.bfloat16)
    low_parts = spread(low_part, "tensor", N_TENSOR)
    partial_value = jnp.dot(grouped, output_weight, preferred_element_type=jnp.float32)
    partial_value = partial_value.astype(jnp.bfloat16).reshape(N_TENSOR, rows, width)
    low = jnp.sum(low_parts.astype(jnp.float32), axis=0).astype(jnp.bfloat16)
    delta = adapter_scale * jnp.dot(low, up, preferred_element_type=jnp.float32)
    delta = delta.astype(jnp.bfloat16).reshape(N_TENSOR, rows, -1)
    received = lax.all_to_all(
        jnp.concatenate([partial_value, delta], axis=2), "tensor", 0, 0
    ).astype(jnp.float32)
    delta = received[:, :, width:].transpose(1, 0, 2).reshape(rows, width)
    reduced = jnp.sum(received[:, :, :width], axis=0) + delta
    return (hidden.astype(jnp.float32) + reduced).astype(jnp.bfloat16)


def solution(mesh):
    in_specs = (
        P(("replica", "tensor"), None),
        P(("replica", "tensor"), None, None, None),
        P(("replica", "tensor"), None, None, None),
        P(("replica", "tensor")),
        P(("replica", "tensor"), None),
        P("tensor", None),
        P("replica", "tensor"),
        P("replica", "tensor"),
    )
    out_specs = P(("replica", "tensor"), None)
    return jax.shard_map(
        per_device, mesh=mesh, in_specs=in_specs, out_specs=out_specs, check_vma=False
    )
```

```python
import math

import jax
import jax.numpy as jnp
from jax import lax
from jax.sharding import PartitionSpec as P

QUERY_HEADS = 64
KVH = 8
HEAD_SIZE = 128
CACHE = 128
GROUP = 8
N_TENSOR = 16
N_REPLICA = 64

adapter_scale = 2.0

SIDE = 4
X_GROUPS = [[y * SIDE + x for x in range(SIDE)] for y in range(SIDE)]
Y_GROUPS = [[y * SIDE + x for y in range(SIDE)] for x in range(SIDE)]
DEPTH = 16
STRIDE = 2
FAR = DEPTH // STRIDE
Z_GROUPS = [
    [(z * STRIDE + low) * 4 + rest for z in range(FAR)]
    for low in range(STRIDE)
    for rest in range(4)
]
HEAD_BITS = (4,)
SUM_BITS = (2, 1)


def attend_rows(queries, stored_keys, stored_values, lengths):
    row_count = queries.shape[0]
    shaped = queries.reshape(row_count, KVH, GROUP, HEAD_SIZE)
    scores = jnp.einsum(
        "rkgd,rksd->rkgs", shaped, stored_keys, preferred_element_type=jnp.float32
    ) / math.sqrt(HEAD_SIZE)
    positions = jnp.arange(CACHE, dtype=jnp.int32)
    visible = positions[None, :] < lengths[:, None]
    scores = jnp.where(visible[:, None, None, :], scores, -1e30)
    highest = jnp.max(scores, axis=-1, keepdims=True)
    expo = jnp.exp(scores - highest)
    denominator = jnp.sum(expo, axis=-1, keepdims=True)
    probs = (expo / denominator).astype(jnp.bfloat16)
    attended = jnp.einsum(
        "rkgs,rksd->rkgd", probs, stored_values, preferred_element_type=jnp.float32
    )
    return attended.astype(jnp.bfloat16).reshape(row_count, QUERY_HEADS * HEAD_SIZE)


def spread(block, axis, count, groups=None):
    copies = jnp.broadcast_to(block[None], (count,) + block.shape)
    return lax.all_to_all(copies, axis, 0, 0, axis_index_groups=groups)


def swap(block, axis, count, bit):
    return lax.ppermute(block, axis, [(i, i ^ bit) for i in range(count)])


def gather_far(adapter_down, adapter_up):
    both = jnp.concatenate([adapter_down, adapter_up], axis=1)
    rank, width = both.shape
    return spread(both, "replica", FAR, Z_GROUPS).reshape(FAR * rank, width)


def gather_near(some, bits):
    for bit in bits:
        other = swap(some, "replica", N_REPLICA, bit)
        some = jnp.concatenate([some, other], axis=0)
    return some


def join_along_x(up, bit):
    other = swap(up, "tensor", N_TENSOR, bit)
    upper = (lax.axis_index("tensor") & bit) == bit
    return jnp.concatenate(
        [jnp.where(upper, other, up), jnp.where(upper, up, other)], axis=1
    )


def per_device(
    queries, stored_keys, stored_values, lengths, hidden, output_weight, adapter_down, adapter_up
):
    rows, width = hidden.shape
    quarter = width // SIDE
    some = gather_far(adapter_down, adapter_up)
    attended = attend_rows(queries, stored_keys, stored_values, lengths)
    blocks = attended.reshape(rows, N_TENSOR, -1).transpose(1, 0, 2)
    some, blocks = lax.optimization_barrier((some, blocks))
    grouped = lax.all_to_all(blocks, "tensor", 0, 0)
    some = gather_near(some, HEAD_BITS)
    grouped = grouped.reshape(SIDE, SIDE, rows, -1).transpose(1, 0, 2, 3)
    grouped = grouped.reshape(N_TENSOR * rows, -1)

    grouped, some = lax.optimization_barrier((grouped, some))
    some = gather_near(some, SUM_BITS)
    partial_value = jnp.dot(grouped, output_weight, preferred_element_type=jnp.float32)
    partial_value = partial_value.astype(jnp.bfloat16)
    down, up = some[:, : adapter_down.shape[1]], some[:, adapter_down.shape[1] :]
    along_x = lax.all_to_all(
        partial_value.reshape(SIDE, SIDE * rows, width),
        "tensor",
        0,
        0,
        axis_index_groups=X_GROUPS,
    )
    low_part = lax.dot_general(
        grouped, down, (((1,), (1,)), ((), ())), preferred_element_type=jnp.float32
    ).astype(jnp.bfloat16)
    low_part = low_part.reshape(1, SIDE, SIDE * rows, -1)
    low_part = jnp.broadcast_to(low_part, (SIDE,) + low_part.shape[1:])
    up = join_along_x(up, 1)
    low_part, along_x, up = lax.optimization_barrier((low_part, along_x, up))
    up_quarter = join_along_x(up, 2)
    low = lax.all_to_all(
        low_part.reshape(N_TENSOR, SIDE * rows, -1), "tensor", 0, 0
    )
    low = jnp.sum(low.astype(jnp.float32), axis=0).astype(jnp.bfloat16)
    delta = adapter_scale * jnp.dot(low, up_quarter, preferred_element_type=jnp.float32)
    summed = jnp.sum(along_x.astype(jnp.float32), axis=0)
    column = lax.broadcasted_iota(jnp.int32, (1, width), 1)
    start = (lax.axis_index("tensor") >> 2) * quarter
    mine = (column >= start) & (column < start + quarter)
    summed = summed + jnp.where(mine, jnp.concatenate([delta] * SIDE, axis=1), 0.0)
    along_y = lax.all_to_all(
        summed.astype(jnp.bfloat16).reshape(SIDE, rows, width),
        "tensor",
        0,
        0,
        axis_index_groups=Y_GROUPS,
    )
    reduced = jnp.sum(along_y.astype(jnp.float32), axis=0)
    return (hidden.astype(jnp.float32) + reduced).astype(jnp.bfloat16)


def solution(mesh):
    in_specs = (
        P(("replica", "tensor"), None),
        P(("replica", "tensor"), None, None, None),
        P(("replica", "tensor"), None, None, None),
        P(("replica", "tensor")),
        P(("replica", "tensor"), None),
        P("tensor", None),
        P("replica", "tensor"),
        P("replica", "tensor"),
    )
    out_specs = P(("replica", "tensor"), None)
    return jax.shard_map(
        per_device, mesh=mesh, in_specs=in_specs, out_specs=out_specs, check_vma=False
    )
```

```python
import math

import jax
import jax.numpy as jnp
from jax import lax
from jax.experimental import pallas as pl
from jax.sharding import PartitionSpec as P

QUERY_HEADS = 64
KVH = 8
HEAD_SIZE = 128
CACHE = 128
GROUP = 8
N_TENSOR = 16
N_REPLICA = 64

adapter_scale = 2.0

DEPTH = 16
Z_GROUPS = [[z * 4 + rest for z in range(DEPTH)] for rest in range(4)]


def attend_rows(queries, stored_keys, stored_values, lengths):
    row_count = queries.shape[0]
    shaped = queries.reshape(row_count, KVH, GROUP, HEAD_SIZE)
    scores = jnp.einsum(
        "rkgd,rksd->rkgs", shaped, stored_keys, preferred_element_type=jnp.float32
    ) / math.sqrt(HEAD_SIZE)
    positions = jnp.arange(CACHE, dtype=jnp.int32)
    visible = positions[None, :] < lengths[:, None]
    scores = jnp.where(visible[:, None, None, :], scores, -1e30)
    highest = jnp.max(scores, axis=-1, keepdims=True)
    expo = jnp.exp(scores - highest)
    denominator = jnp.sum(expo, axis=-1, keepdims=True)
    probs = (expo / denominator).astype(jnp.bfloat16)
    attended = jnp.einsum(
        "rkgs,rksd->rkgd", probs, stored_values, preferred_element_type=jnp.float32
    )
    return attended.astype(jnp.bfloat16).reshape(row_count, QUERY_HEADS * HEAD_SIZE)


def spread(block, axis, count, groups=None):
    copies = jnp.broadcast_to(block[None], (count,) + block.shape)
    return lax.all_to_all(copies, axis, 0, 0, axis_index_groups=groups)


def swap(block, axis, count, bit):
    return lax.ppermute(block, axis, [(i, i ^ bit) for i in range(count)])


def gather_along_z(adapter_down, adapter_up):
    rank, split = adapter_down.shape
    width = split + adapter_up.shape[1]

    def copy_out(down_ref, up_ref, copies_ref):
        for peer in range(DEPTH):
            copies_ref[peer, :, :split] = down_ref[...]
            copies_ref[peer, :, split:] = up_ref[...]

    copies = pl.pallas_call(
        copy_out, out_shape=jax.ShapeDtypeStruct((DEPTH, rank, width), adapter_down.dtype)
    )(adapter_down, adapter_up)
    every = lax.all_to_all(copies, "replica", 0, 0, axis_index_groups=Z_GROUPS)
    return every.reshape(DEPTH * rank, width)


def gather_rest(some, split):
    for bit in (1, 2):
        other = swap(some, "replica", N_REPLICA, bit)
        some = jnp.concatenate([some, other], axis=0)
    return some[:, :split], some[:, split:]


def per_device(
    queries, stored_keys, stored_values, lengths, hidden, output_weight, adapter_down, adapter_up
):
    rows, width = hidden.shape
    some = gather_along_z(adapter_down, adapter_up)
    attended = attend_rows(queries, stored_keys, stored_values, lengths)
    blocks = attended.reshape(rows, N_TENSOR, -1).transpose(1, 0, 2)
    some, blocks = lax.optimization_barrier((some, blocks))
    down, up = gather_rest(some, adapter_down.shape[1])
    grouped = lax.all_to_all(blocks, "tensor", 0, 0).reshape(N_TENSOR * rows, -1)

    low_part = lax.dot_general(
        grouped, down, (((1,), (1,)), ((), ())), preferred_element_type=jnp.float32
    ).astype(jnp.bfloat16)
    low_parts = spread(low_part, "tensor", N_TENSOR)
    partial_value = jnp.dot(grouped, output_weight, preferred_element_type=jnp.float32)
    partial_value = partial_value.astype(jnp.bfloat16).reshape(N_TENSOR, rows, width)
    residual, low_parts = lax.optimization_barrier((hidden.astype(jnp.float32), low_parts))
    low = jnp.sum(low_parts.astype(jnp.float32), axis=0).astype(jnp.bfloat16)
    delta = adapter_scale * jnp.dot(low, up, preferred_element_type=jnp.float32)
    delta = delta.astype(jnp.bfloat16).reshape(N_TENSOR, rows, -1)
    received = lax.all_to_all(
        jnp.concatenate([partial_value, delta], axis=2), "tensor", 0, 0
    ).astype(jnp.float32)
    delta = received[:, :, width:].transpose(1, 0, 2).reshape(rows, width)
    reduced = jnp.sum(received[:, :, :width], axis=0) + delta
    return (residual + reduced).astype(jnp.bfloat16)


def solution(mesh):
    in_specs = (
        P(("replica", "tensor"), None),
        P(("replica", "tensor"), None, None, None),
        P(("replica", "tensor"), None, None, None),
        P(("replica", "tensor")),
        P(("replica", "tensor"), None),
        P("tensor", None),
        P("replica", "tensor"),
        P("replica", "tensor"),
    )
    out_specs = P(("replica", "tensor"), None)
    return jax.shard_map(
        per_device, mesh=mesh, in_specs=in_specs, out_specs=out_specs, check_vma=False
    )
```

```python
import math

import jax
import jax.numpy as jnp
from jax import lax
from jax.sharding import PartitionSpec as P

QUERY_HEADS = 64
KVH = 8
HEAD_SIZE = 128
CACHE = 128
GROUP = 8
N_TENSOR = 16
N_REPLICA = 64

adapter_scale = 2.0

HALF = 8
HALF_GROUPS = [[upper * HALF + near for near in range(HALF)] for upper in range(2)]
DEPTH = 16
Z_GROUPS = [[z * 4 + rest for z in range(DEPTH)] for rest in range(4)]


def attend_rows(queries, stored_keys, stored_values, lengths):
    row_count = queries.shape[0]
    shaped = queries.reshape(row_count, KVH, GROUP, HEAD_SIZE)
    scores = jnp.einsum(
        "rkgd,rksd->rkgs", shaped, stored_keys, preferred_element_type=jnp.float32
    ) / math.sqrt(HEAD_SIZE)
    positions = jnp.arange(CACHE, dtype=jnp.int32)
    visible = positions[None, :] < lengths[:, None]
    scores = jnp.where(visible[:, None, None, :], scores, -1e30)
    highest = jnp.max(scores, axis=-1, keepdims=True)
    expo = jnp.exp(scores - highest)
    denominator = jnp.sum(expo, axis=-1, keepdims=True)
    probs = (expo / denominator).astype(jnp.bfloat16)
    attended = jnp.einsum(
        "rkgs,rksd->rkgd", probs, stored_values, preferred_element_type=jnp.float32
    )
    return attended.astype(jnp.bfloat16).reshape(row_count, QUERY_HEADS * HEAD_SIZE)


def spread(block, axis, count, groups=None):
    copies = jnp.broadcast_to(block[None], (count,) + block.shape)
    return lax.all_to_all(copies, axis, 0, 0, axis_index_groups=groups)


def swap(block, axis, count, bit):
    return lax.ppermute(block, axis, [(i, i ^ bit) for i in range(count)])


def gather_along_z(adapter_down, adapter_up):
    both = jnp.concatenate([adapter_down, adapter_up], axis=1)
    rank, width = both.shape
    return spread(both, "replica", DEPTH, Z_GROUPS).reshape(DEPTH * rank, width)


def gather_rest(some, split):
    for bit in (2, 1):
        other = swap(some, "replica", N_REPLICA, bit)
        some = jnp.concatenate([some, other], axis=0)
    return some[:, :split], some[:, split:]


def per_device(
    queries, stored_keys, stored_values, lengths, hidden, output_weight, adapter_down, adapter_up
):
    rows, width = hidden.shape
    some = gather_along_z(adapter_down, adapter_up)
    attended = attend_rows(queries, stored_keys, stored_values, lengths)
    blocks = attended.reshape(rows, N_TENSOR, -1).transpose(1, 0, 2)
    some, blocks = lax.optimization_barrier((some, blocks))
    down, up = gather_rest(some, adapter_down.shape[1])
    grouped = lax.all_to_all(blocks, "tensor", 0, 0)
    grouped = grouped.reshape(2, HALF, rows, -1).transpose(1, 0, 2, 3)
    grouped = grouped.reshape(N_TENSOR * rows, -1)

    low_part = lax.dot_general(
        grouped, down, (((1,), (1,)), ((), ())), preferred_element_type=jnp.float32
    ).astype(jnp.bfloat16)
    low_parts = spread(low_part, "tensor", N_TENSOR)
    partial_value = jnp.dot(grouped, output_weight, preferred_element_type=jnp.float32)
    partial_value = partial_value.astype(jnp.bfloat16).reshape(HALF, 2 * rows, width)
    residual, low_parts = lax.optimization_barrier((hidden.astype(jnp.float32), low_parts))
    low = jnp.sum(low_parts.astype(jnp.float32), axis=0).astype(jnp.bfloat16)
    delta = adapter_scale * jnp.dot(low, up, preferred_element_type=jnp.float32)
    delta = delta.astype(jnp.bfloat16).reshape(HALF, 2 * rows, -1)
    received = lax.all_to_all(
        jnp.concatenate([partial_value, delta], axis=2),
        "tensor",
        0,
        0,
        axis_index_groups=HALF_GROUPS,
    ).astype(jnp.float32)
    upper = lax.axis_index("tensor") >= HALF
    delta = received[:, :, width:].transpose(1, 0, 2).reshape(2 * rows, width // 2)
    delta = jnp.concatenate(
        [jnp.where(upper, 0.0, delta), jnp.where(upper, delta, 0.0)], axis=1
    )
    reduced = jnp.sum(received[:, :, :width], axis=0) + delta
    kept = jnp.where(upper, reduced[rows:], reduced[:rows])
    sent = jnp.where(upper, reduced[:rows], reduced[rows:]).astype(jnp.bfloat16)
    other = swap(sent, "tensor", N_TENSOR, HALF)
    return (residual + kept + other.astype(jnp.float32)).astype(jnp.bfloat16)


def solution(mesh):
    in_specs = (
        P(("replica", "tensor"), None),
        P(("replica", "tensor"), None, None, None),
        P(("replica", "tensor"), None, None, None),
        P(("replica", "tensor")),
        P(("replica", "tensor"), None),
        P("tensor", None),
        P("replica", "tensor"),
        P("replica", "tensor"),
    )
    out_specs = P(("replica", "tensor"), None)
    return jax.shard_map(
        per_device, mesh=mesh, in_specs=in_specs, out_specs=out_specs, check_vma=False
    )
```

```python
import math

import jax
import jax.numpy as jnp
from jax import lax
from jax.sharding import PartitionSpec as P

QUERY_HEADS = 64
KVH = 8
HEAD_SIZE = 128
CACHE = 128
GROUP = 8
N_TENSOR = 16
N_REPLICA = 64

adapter_scale = 2.0

HALF = 8
HALF_GROUPS = [[upper * HALF + near for near in range(HALF)] for upper in range(2)]
DEPTH = 16
Z_GROUPS = [[z * 4 + rest for z in range(DEPTH)] for rest in range(4)]


def attend_rows(queries, stored_keys, stored_values, lengths):
    row_count = queries.shape[0]
    shaped = queries.reshape(row_count, KVH, GROUP, HEAD_SIZE)
    scores = jnp.einsum(
        "rkgd,rksd->rkgs", shaped, stored_keys, preferred_element_type=jnp.float32
    ) / math.sqrt(HEAD_SIZE)
    positions = jnp.arange(CACHE, dtype=jnp.int32)
    visible = positions[None, :] < lengths[:, None]
    scores = jnp.where(visible[:, None, None, :], scores, -1e30)
    highest = jnp.max(scores, axis=-1, keepdims=True)
    expo = jnp.exp(scores - highest)
    denominator = jnp.sum(expo, axis=-1, keepdims=True)
    probs = (expo / denominator).astype(jnp.bfloat16)
    attended = jnp.einsum(
        "rkgs,rksd->rkgd", probs, stored_values, preferred_element_type=jnp.float32
    )
    return attended.astype(jnp.bfloat16).reshape(row_count, QUERY_HEADS * HEAD_SIZE)


def spread(block, axis, count, groups=None):
    copies = jnp.broadcast_to(block[None], (count,) + block.shape)
    return lax.all_to_all(copies, axis, 0, 0, axis_index_groups=groups)


def swap(block, axis, count, bit):
    return lax.ppermute(block, axis, [(i, i ^ bit) for i in range(count)])


def gather_along_z(adapter_down, adapter_up):
    both = jnp.concatenate([adapter_down, adapter_up], axis=1)
    rank, width = both.shape
    return spread(both, "replica", DEPTH, Z_GROUPS).reshape(DEPTH * rank, width)


def gather_rest(some, split):
    for bit in (2, 1):
        other = swap(some, "replica", N_REPLICA, bit)
        some = jnp.concatenate([some, other], axis=0)
    return some[:, :split], some[:, split:]


def per_device(
    queries, stored_keys, stored_values, lengths, hidden, output_weight, adapter_down, adapter_up
):
    rows, width = hidden.shape
    some = gather_along_z(adapter_down, adapter_up)
    attended = attend_rows(queries, stored_keys, stored_values, lengths)
    blocks = attended.reshape(rows, N_TENSOR, -1).transpose(1, 0, 2)
    some, blocks = lax.optimization_barrier((some, blocks))
    down, up = gather_rest(some, adapter_down.shape[1])
    grouped = lax.all_to_all(blocks, "tensor", 0, 0)
    grouped = grouped.reshape(2, HALF, rows, -1).transpose(1, 0, 2, 3)
    grouped = grouped.reshape(N_TENSOR * rows, -1)

    low_part = lax.dot_general(
        grouped, down, (((1,), (1,)), ((), ())), preferred_element_type=jnp.float32
    ).astype(jnp.bfloat16)
    low_parts = spread(low_part, "tensor", HALF, HALF_GROUPS)
    upper = lax.axis_index("tensor") >= HALF
    other = swap(up, "tensor", N_TENSOR, HALF)
    other, grouped = lax.optimization_barrier((other, grouped))
    up = jnp.concatenate([jnp.where(upper, other, up), jnp.where(upper, up, other)], axis=1)
    partial_value = jnp.dot(grouped, output_weight, preferred_element_type=jnp.float32)
    partial_value = partial_value.astype(jnp.bfloat16).reshape(HALF, 2 * rows, width)
    residual, low_parts = lax.optimization_barrier((hidden.astype(jnp.float32), low_parts))
    low = jnp.sum(low_parts.astype(jnp.float32), axis=0).astype(jnp.bfloat16)
    delta = adapter_scale * jnp.dot(low, up, preferred_element_type=jnp.float32)
    delta = delta.astype(jnp.bfloat16).reshape(HALF, 2 * rows, -1)
    received = lax.all_to_all(
        jnp.concatenate([partial_value, delta], axis=2),
        "tensor",
        0,
        0,
        axis_index_groups=HALF_GROUPS,
    ).astype(jnp.float32)
    delta = received[:, :, width:].reshape(HALF, 2 * rows, 2, -1).transpose(1, 2, 0, 3)
    reduced = jnp.sum(received[:, :, :width], axis=0) + delta.reshape(2 * rows, width)
    kept = jnp.where(upper, reduced[rows:], reduced[:rows])
    sent = jnp.where(upper, reduced[:rows], reduced[rows:]).astype(jnp.bfloat16)
    other = swap(sent, "tensor", N_TENSOR, HALF)
    return (residual + kept + other.astype(jnp.float32)).astype(jnp.bfloat16)


def solution(mesh):
    in_specs = (
        P(("replica", "tensor"), None),
        P(("replica", "tensor"), None, None, None),
        P(("replica", "tensor"), None, None, None),
        P(("replica", "tensor")),
        P(("replica", "tensor"), None),
        P("tensor", None),
        P("replica", "tensor"),
        P("replica", "tensor"),
    )
    out_specs = P(("replica", "tensor"), None)
    return jax.shard_map(
        per_device, mesh=mesh, in_specs=in_specs, out_specs=out_specs, check_vma=False
    )
```

```python
import math

import jax
import jax.numpy as jnp
from jax import lax
from jax.sharding import PartitionSpec as P

QUERY_HEADS = 64
KVH = 8
HEAD_SIZE = 128
CACHE = 128
GROUP = 8
N_TENSOR = 16
N_REPLICA = 64

adapter_scale = 2.0

HALF = 8
HALF_GROUPS = [[upper * HALF + near for near in range(HALF)] for upper in range(2)]
DEPTH = 16
Z_GROUPS = [[z * 4 + rest for z in range(DEPTH)] for rest in range(4)]


def attend_rows(queries, stored_keys, stored_values, lengths):
    row_count = queries.shape[0]
    shaped = queries.reshape(row_count, KVH, GROUP, HEAD_SIZE)
    scores = jnp.einsum(
        "rkgd,rksd->rkgs", shaped, stored_keys, preferred_element_type=jnp.float32
    ) / math.sqrt(HEAD_SIZE)
    positions = jnp.arange(CACHE, dtype=jnp.int32)
    visible = positions[None, :] < lengths[:, None]
    scores = jnp.where(visible[:, None, None, :], scores, -1e30)
    highest = jnp.max(scores, axis=-1, keepdims=True)
    expo = jnp.exp(scores - highest)
    denominator = jnp.sum(expo, axis=-1, keepdims=True)
    probs = (expo / denominator).astype(jnp.bfloat16)
    attended = jnp.einsum(
        "rkgs,rksd->rkgd", probs, stored_values, preferred_element_type=jnp.float32
    )
    return attended.astype(jnp.bfloat16).reshape(row_count, QUERY_HEADS * HEAD_SIZE)


def spread(block, axis, count, groups=None):
    copies = jnp.broadcast_to(block[None], (count,) + block.shape)
    return lax.all_to_all(copies, axis, 0, 0, axis_index_groups=groups)


def swap(block, axis, count, bit):
    return lax.ppermute(block, axis, [(i, i ^ bit) for i in range(count)])


def gather_along_z(adapter_down, adapter_up):
    both = jnp.concatenate([adapter_down, adapter_up], axis=1)
    rank, width = both.shape
    return spread(both, "replica", DEPTH, Z_GROUPS).reshape(DEPTH * rank, width)


def gather_rest(some, split):
    for bit in (2, 1):
        other = swap(some, "replica", N_REPLICA, bit)
        some = jnp.concatenate([some, other], axis=0)
    return some[:, :split], some[:, split:]


def per_device(
    queries, stored_keys, stored_values, lengths, hidden, output_weight, adapter_down, adapter_up
):
    rows, width = hidden.shape
    some = gather_along_z(adapter_down, adapter_up)
    attended = attend_rows(queries, stored_keys, stored_values, lengths)
    blocks = attended.reshape(rows, N_TENSOR, -1).transpose(1, 0, 2)
    some, blocks = lax.optimization_barrier((some, blocks))
    down, up = gather_rest(some, adapter_down.shape[1])
    grouped = lax.all_to_all(blocks, "tensor", 0, 0)
    grouped = grouped.reshape(2, HALF, rows, -1).transpose(1, 0, 2, 3)
    grouped = grouped.reshape(N_TENSOR * rows, -1)

    low_part = lax.dot_general(
        down, grouped, (((1,), (1,)), ((), ())), preferred_element_type=jnp.float32
    ).astype(jnp.bfloat16)
    by_rank = jnp.concatenate([low_part, up], axis=1)
    by_rank = lax.all_to_all(by_rank.reshape(N_TENSOR, -1, by_rank.shape[1]), "tensor", 0, 0)
    partial_value = jnp.dot(grouped, output_weight, preferred_element_type=jnp.float32)
    residual, by_rank = lax.optimization_barrier((hidden.astype(jnp.float32), by_rank))
    low = jnp.sum(by_rank[:, :, : N_TENSOR * rows].astype(jnp.float32), axis=0)
    up = by_rank[:, :, N_TENSOR * rows :].transpose(1, 0, 2).reshape(-1, width)
    delta = lax.dot_general(
        low.astype(jnp.bfloat16), up, (((0,), (0,)), ((), ())), preferred_element_type=jnp.float32
    )
    partial_value = (partial_value + adapter_scale * delta).astype(jnp.bfloat16)
    received = lax.all_to_all(
        partial_value.reshape(HALF, 2 * rows, width),
        "tensor",
        0,
        0,
        axis_index_groups=HALF_GROUPS,
    )
    reduced = jnp.sum(received.astype(jnp.float32), axis=0)
    upper = lax.axis_index("tensor") >= HALF
    kept = jnp.where(upper, reduced[rows:], reduced[:rows])
    sent = jnp.where(upper, reduced[:rows], reduced[rows:]).astype(jnp.bfloat16)
    other = swap(sent, "tensor", N_TENSOR, HALF)
    return (residual + kept + other.astype(jnp.float32)).astype(jnp.bfloat16)


def solution(mesh):
    in_specs = (
        P(("replica", "tensor"), None),
        P(("replica", "tensor"), None, None, None),
        P(("replica", "tensor"), None, None, None),
        P(("replica", "tensor")),
        P(("replica", "tensor"), None),
        P("tensor", None),
        P("replica", "tensor"),
        P("replica", "tensor"),
    )
    out_specs = P(("replica", "tensor"), None)
    return jax.shard_map(
        per_device, mesh=mesh, in_specs=in_specs, out_specs=out_specs, check_vma=False
    )
```

```python
import math

import jax
import jax.numpy as jnp
from jax import lax
from jax.sharding import PartitionSpec as P

QUERY_HEADS = 64
KVH = 8
HEAD_SIZE = 128
CACHE = 128
GROUP = 8
N_TENSOR = 16
N_REPLICA = 64

adapter_scale = 2.0

HALF = 8
HALF_GROUPS = [[upper * HALF + near for near in range(HALF)] for upper in range(2)]
DEPTH = 16
Z_GROUPS = [[z * 4 + rest for z in range(DEPTH)] for rest in range(4)]


def attend_rows(queries, stored_keys, stored_values, lengths):
    row_count = queries.shape[0]
    shaped = queries.reshape(row_count, KVH, GROUP, HEAD_SIZE)
    scores = jnp.einsum(
        "rkgd,rksd->rkgs", shaped, stored_keys, preferred_element_type=jnp.float32
    ) / math.sqrt(HEAD_SIZE)
    positions = jnp.arange(CACHE, dtype=jnp.int32)
    visible = positions[None, :] < lengths[:, None]
    scores = jnp.where(visible[:, None, None, :], scores, -1e30)
    highest = jnp.max(scores, axis=-1, keepdims=True)
    expo = jnp.exp(scores - highest)
    denominator = jnp.sum(expo, axis=-1, keepdims=True)
    probs = (expo / denominator).astype(jnp.bfloat16)
    attended = jnp.einsum(
        "rkgs,rksd->rkgd", probs, stored_values, preferred_element_type=jnp.float32
    )
    return attended.astype(jnp.bfloat16).reshape(row_count, QUERY_HEADS * HEAD_SIZE)


def spread(block, axis, count, groups=None):
    copies = jnp.broadcast_to(block[None], (count,) + block.shape)
    return lax.all_to_all(copies, axis, 0, 0, axis_index_groups=groups)


def swap(block, axis, count, bit):
    return lax.ppermute(block, axis, [(i, i ^ bit) for i in range(count)])


def gather_along_z(adapter_down, adapter_up):
    both = jnp.concatenate([adapter_down, adapter_up], axis=1)
    both = jnp.concatenate([both, swap(both, "replica", N_REPLICA, 2)], axis=0)
    rank, width = both.shape
    return spread(both, "replica", DEPTH, Z_GROUPS).reshape(DEPTH * rank, width)


def gather_rest(some, split):
    some = jnp.concatenate([some, swap(some, "replica", N_REPLICA, 1)], axis=0)
    return some[:, :split], some[:, split:]


def per_device(
    queries, stored_keys, stored_values, lengths, hidden, output_weight, adapter_down, adapter_up
):
    rows, width = hidden.shape
    some = gather_along_z(adapter_down, adapter_up)
    attended = attend_rows(queries, stored_keys, stored_values, lengths)
    blocks = attended.reshape(rows, N_TENSOR, -1).transpose(1, 0, 2)
    some, blocks = lax.optimization_barrier((some, blocks))
    down, up = gather_rest(some, adapter_down.shape[1])
    grouped = lax.all_to_all(blocks, "tensor", 0, 0)
    grouped = grouped.reshape(2, HALF, rows, -1).transpose(1, 0, 2, 3)
    grouped = grouped.reshape(N_TENSOR * rows, -1)

    low_part = lax.dot_general(
        down, grouped, (((1,), (1,)), ((), ())), preferred_element_type=jnp.float32
    ).astype(jnp.bfloat16)
    by_rank = jnp.concatenate([low_part, up], axis=1)
    by_rank = lax.all_to_all(by_rank.reshape(N_TENSOR, -1, by_rank.shape[1]), "tensor", 0, 0)
    partial_value = jnp.dot(grouped, output_weight, preferred_element_type=jnp.float32)
    residual, by_rank = lax.optimization_barrier((hidden.astype(jnp.float32), by_rank))
    low = jnp.sum(by_rank[:, :, : N_TENSOR * rows].astype(jnp.float32), axis=0)
    up = by_rank[:, :, N_TENSOR * rows :].transpose(1, 0, 2).reshape(-1, width)
    delta = lax.dot_general(
        low.astype(jnp.bfloat16), up, (((0,), (0,)), ((), ())), preferred_element_type=jnp.float32
    )
    partial_value = (partial_value + adapter_scale * delta).astype(jnp.bfloat16)
    received = lax.all_to_all(
        partial_value.reshape(HALF, 2 * rows, width),
        "tensor",
        0,
        0,
        axis_index_groups=HALF_GROUPS,
    )
    reduced = jnp.sum(received.astype(jnp.float32), axis=0)
    upper = lax.axis_index("tensor") >= HALF
    kept = jnp.where(upper, reduced[rows:], reduced[:rows])
    sent = jnp.where(upper, reduced[:rows], reduced[rows:]).astype(jnp.bfloat16)
    other = swap(sent, "tensor", N_TENSOR, HALF)
    return (residual + kept + other.astype(jnp.float32)).astype(jnp.bfloat16)


def solution(mesh):
    in_specs = (
        P(("replica", "tensor"), None),
        P(("replica", "tensor"), None, None, None),
        P(("replica", "tensor"), None, None, None),
        P(("replica", "tensor")),
        P(("replica", "tensor"), None),
        P("tensor", None),
        P("replica", "tensor"),
        P("replica", "tensor"),
    )
    out_specs = P(("replica", "tensor"), None)
    return jax.shard_map(
        per_device, mesh=mesh, in_specs=in_specs, out_specs=out_specs, check_vma=False
    )
```

```python
import math

import jax
import jax.numpy as jnp
from jax import lax
from jax.sharding import PartitionSpec as P

QUERY_HEADS = 64
KVH = 8
HEAD_SIZE = 128
CACHE = 128
GROUP = 8
N_TENSOR = 16
N_REPLICA = 64

adapter_scale = 2.0

NEAR_Y = 4
PAIRS = [upper * 8 + x for upper in range(2) for x in range(4)]
PLACE_GROUPS = [[near + pair for near in (0, NEAR_Y) for pair in PAIRS]]
ACROSS_GROUPS = [[near + pair for pair in PAIRS] for near in (0, NEAR_Y)]
DEPTH = 16
Z_GROUPS = [[z * 4 + rest for z in range(DEPTH)] for rest in range(4)]


def attend_rows(queries, stored_keys, stored_values, lengths):
    row_count = queries.shape[0]
    shaped = queries.reshape(row_count, KVH, GROUP, HEAD_SIZE)
    scores = jnp.einsum(
        "rkgd,rksd->rkgs", shaped, stored_keys, preferred_element_type=jnp.float32
    ) / math.sqrt(HEAD_SIZE)
    positions = jnp.arange(CACHE, dtype=jnp.int32)
    visible = positions[None, :] < lengths[:, None]
    scores = jnp.where(visible[:, None, None, :], scores, -1e30)
    highest = jnp.max(scores, axis=-1, keepdims=True)
    expo = jnp.exp(scores - highest)
    denominator = jnp.sum(expo, axis=-1, keepdims=True)
    probs = (expo / denominator).astype(jnp.bfloat16)
    attended = jnp.einsum(
        "rkgs,rksd->rkgd", probs, stored_values, preferred_element_type=jnp.float32
    )
    return attended.astype(jnp.bfloat16).reshape(row_count, QUERY_HEADS * HEAD_SIZE)


def spread(block, axis, count, groups=None):
    copies = jnp.broadcast_to(block[None], (count,) + block.shape)
    return lax.all_to_all(copies, axis, 0, 0, axis_index_groups=groups)


def swap(block, axis, count, bit):
    return lax.ppermute(block, axis, [(i, i ^ bit) for i in range(count)])


def gather_along_z(adapter_down, adapter_up):
    both = jnp.concatenate([adapter_down, adapter_up], axis=1)
    rank, width = both.shape
    return spread(both, "replica", DEPTH, Z_GROUPS).reshape(DEPTH * rank, width)


def gather_rest(some, split):
    for bit in (2, 1):
        other = swap(some, "replica", N_REPLICA, bit)
        some = jnp.concatenate([some, other], axis=0)
    return some[:, :split], some[:, split:]


def per_device(
    queries, stored_keys, stored_values, lengths, hidden, output_weight, adapter_down, adapter_up
):
    rows, width = hidden.shape
    some = gather_along_z(adapter_down, adapter_up)
    attended = attend_rows(queries, stored_keys, stored_values, lengths)
    blocks = attended.reshape(rows, 2, 2, 4, -1).transpose(2, 1, 3, 0, 4)
    blocks = blocks.reshape(N_TENSOR, rows, -1)
    some, blocks = lax.optimization_barrier((some, blocks))
    down, up = gather_rest(some, adapter_down.shape[1])
    grouped = lax.all_to_all(blocks, "tensor", 0, 0, axis_index_groups=PLACE_GROUPS)
    grouped = grouped.reshape(N_TENSOR * rows, -1)
    half = N_TENSOR * rows // 2

    low_part = lax.dot_general(
        down, grouped, (((1,), (1,)), ((), ())), preferred_element_type=jnp.float32
    ).astype(jnp.bfloat16)
    low_part = low_part.reshape(len(PAIRS), -1, 2, half).transpose(2, 0, 1, 3)
    up = up.reshape(1, len(PAIRS), -1, up.shape[1])
    up = jnp.broadcast_to(up, (2,) + up.shape[1:])
    by_rank = jnp.concatenate([low_part, up], axis=3)
    by_rank = lax.all_to_all(
        by_rank.reshape(N_TENSOR, -1, by_rank.shape[3]),
        "tensor",
        0,
        0,
        axis_index_groups=PLACE_GROUPS,
    )
    partial_value = jnp.dot(grouped, output_weight, preferred_element_type=jnp.float32)
    start = jnp.where((lax.axis_index("tensor") & NEAR_Y) == NEAR_Y, half, 0)
    kept = lax.dynamic_slice_in_dim(partial_value, start, half, 0)
    sent = lax.dynamic_slice_in_dim(partial_value, half - start, half, 0)
    other = swap(sent.astype(jnp.bfloat16), "tensor", N_TENSOR, NEAR_Y)

    residual, by_rank = lax.optimization_barrier((hidden.astype(jnp.float32), by_rank))
    low = jnp.sum(by_rank[:, :, :half].astype(jnp.float32), axis=0)
    up = by_rank[:, :, half:]
    up = up.reshape(2, 2, 4, up.shape[1], -1).transpose(3, 1, 0, 2, 4).reshape(-1, width)
    delta = lax.dot_general(
        low.astype(jnp.bfloat16), up, (((0,), (0,)), ((), ())), preferred_element_type=jnp.float32
    )
    kept = (kept + other.astype(jnp.float32) + adapter_scale * delta).astype(jnp.bfloat16)
    received = lax.all_to_all(
        kept.reshape(len(PAIRS), rows, width), "tensor", 0, 0, axis_index_groups=ACROSS_GROUPS
    )
    reduced = jnp.sum(received.astype(jnp.float32), axis=0)
    return (residual + reduced).astype(jnp.bfloat16)


def solution(mesh):
    in_specs = (
        P(("replica", "tensor"), None),
        P(("replica", "tensor"), None, None, None),
        P(("replica", "tensor"), None, None, None),
        P(("replica", "tensor")),
        P(("replica", "tensor"), None),
        P("tensor", None),
        P("replica", "tensor"),
        P("replica", "tensor"),
    )
    out_specs = P(("replica", "tensor"), None)
    return jax.shard_map(
        per_device, mesh=mesh, in_specs=in_specs, out_specs=out_specs, check_vma=False
    )
```

```python
import math

import jax
import jax.numpy as jnp
from jax import lax
from jax.sharding import PartitionSpec as P

QUERY_HEADS = 64
KVH = 8
HEAD_SIZE = 128
CACHE = 128
GROUP = 8
N_TENSOR = 16
N_REPLICA = 64

adapter_scale = 2.0

HALF = 8
PLACE_GROUPS = [[half * HALF + near for near in range(HALF) for half in range(2)]]
HALF_GROUPS = [[upper * HALF + near for near in range(HALF)] for upper in range(2)]
DEPTH = 16
Z_GROUPS = [[z * 4 + rest for z in range(DEPTH)] for rest in range(4)]


def attend_rows(queries, stored_keys, stored_values, lengths):
    row_count = queries.shape[0]
    shaped = queries.reshape(row_count, KVH, GROUP, HEAD_SIZE)
    scores = jnp.einsum(
        "rkgd,rksd->rkgs", shaped, stored_keys, preferred_element_type=jnp.float32
    ) / math.sqrt(HEAD_SIZE)
    positions = jnp.arange(CACHE, dtype=jnp.int32)
    visible = positions[None, :] < lengths[:, None]
    scores = jnp.where(visible[:, None, None, :], scores, -1e30)
    highest = jnp.max(scores, axis=-1, keepdims=True)
    expo = jnp.exp(scores - highest)
    denominator = jnp.sum(expo, axis=-1, keepdims=True)
    probs = (expo / denominator).astype(jnp.bfloat16)
    attended = jnp.einsum(
        "rkgs,rksd->rkgd", probs, stored_values, preferred_element_type=jnp.float32
    )
    return attended.astype(jnp.bfloat16).reshape(row_count, QUERY_HEADS * HEAD_SIZE)


def spread(block, axis, count, groups=None):
    copies = jnp.broadcast_to(block[None], (count,) + block.shape)
    return lax.all_to_all(copies, axis, 0, 0, axis_index_groups=groups)


def swap(block, axis, count, bit):
    return lax.ppermute(block, axis, [(i, i ^ bit) for i in range(count)])


def gather_along_z(adapter_down, adapter_up):
    both = jnp.concatenate([adapter_down, adapter_up], axis=1)
    rank, width = both.shape
    return spread(both, "replica", DEPTH, Z_GROUPS).reshape(DEPTH * rank, width)


def gather_rest(some, split):
    for bit in (2, 1):
        other = swap(some, "replica", N_REPLICA, bit)
        some = jnp.concatenate([some, other], axis=0)
    return some[:, :split], some[:, split:]


def per_device(
    queries, stored_keys, stored_values, lengths, hidden, output_weight, adapter_down, adapter_up
):
    rows, width = hidden.shape
    some = gather_along_z(adapter_down, adapter_up)
    attended = attend_rows(queries, stored_keys, stored_values, lengths)
    blocks = attended.reshape(rows, 2, HALF, -1).transpose(2, 1, 0, 3)
    blocks = blocks.reshape(N_TENSOR, rows, -1)
    some, blocks = lax.optimization_barrier((some, blocks))
    down, up = gather_rest(some, adapter_down.shape[1])
    grouped = lax.all_to_all(blocks, "tensor", 0, 0, axis_index_groups=PLACE_GROUPS)
    grouped = grouped.reshape(N_TENSOR * rows, -1)

    low_part = lax.dot_general(
        down, grouped, (((1,), (1,)), ((), ())), preferred_element_type=jnp.float32
    ).astype(jnp.bfloat16)
    by_rank = jnp.concatenate([low_part, up], axis=1)
    by_rank = lax.all_to_all(by_rank.reshape(N_TENSOR, -1, by_rank.shape[1]), "tensor", 0, 0)
    partial_value = jnp.dot(grouped, output_weight, preferred_element_type=jnp.float32)
    residual, upper, by_rank = lax.optimization_barrier(
        (hidden.astype(jnp.float32), lax.axis_index("tensor") >= HALF, by_rank)
    )
    low = jnp.sum(by_rank[:, :, : N_TENSOR * rows].astype(jnp.float32), axis=0)
    up = by_rank[:, :, N_TENSOR * rows :].transpose(1, 0, 2).reshape(-1, width)
    delta = lax.dot_general(
        low.astype(jnp.bfloat16), up, (((0,), (0,)), ((), ())), preferred_element_type=jnp.float32
    )
    partial_value = (partial_value + adapter_scale * delta).astype(jnp.bfloat16)
    received = lax.all_to_all(
        partial_value.reshape(HALF, 2 * rows, width),
        "tensor",
        0,
        0,
        axis_index_groups=HALF_GROUPS,
    )
    reduced = jnp.sum(received.astype(jnp.float32), axis=0)
    kept = jnp.where(upper, reduced[rows:], reduced[:rows])
    sent = jnp.where(upper, reduced[:rows], reduced[rows:]).astype(jnp.bfloat16)
    other = swap(sent, "tensor", N_TENSOR, HALF)
    return (residual + kept + other.astype(jnp.float32)).astype(jnp.bfloat16)


def solution(mesh):
    in_specs = (
        P(("replica", "tensor"), None),
        P(("replica", "tensor"), None, None, None),
        P(("replica", "tensor"), None, None, None),
        P(("replica", "tensor")),
        P(("replica", "tensor"), None),
        P("tensor", None),
        P("replica", "tensor"),
        P("replica", "tensor"),
    )
    out_specs = P(("replica", "tensor"), None)
    return jax.shard_map(
        per_device, mesh=mesh, in_specs=in_specs, out_specs=out_specs, check_vma=False
    )
```

```python
import math

import jax
import jax.numpy as jnp
from jax import lax
from jax.sharding import PartitionSpec as P

QUERY_HEADS = 64
KVH = 8
HEAD_SIZE = 128
CACHE = 128
GROUP = 8
N_TENSOR = 16
N_REPLICA = 64

adapter_scale = 2.0

HALF = 8
PLACE_GROUPS = [[half * HALF + near for near in range(HALF) for half in range(2)]]
HALF_GROUPS = [[upper * HALF + near for near in range(HALF)] for upper in range(2)]
DEPTH = 16
Z_GROUPS = [[z * 4 + rest for z in range(DEPTH)] for rest in range(4)]


def attend_rows(queries, stored_keys, stored_values, lengths):
    row_count = queries.shape[0]
    shaped = queries.reshape(row_count, KVH, GROUP, HEAD_SIZE)
    scores = jnp.einsum(
        "rkgd,rksd->rkgs", shaped, stored_keys, preferred_element_type=jnp.float32
    ) / math.sqrt(HEAD_SIZE)
    positions = jnp.arange(CACHE, dtype=jnp.int32)
    visible = positions[None, :] < lengths[:, None]
    scores = jnp.where(visible[:, None, None, :], scores, -1e30)
    highest = jnp.max(scores, axis=-1, keepdims=True)
    expo = jnp.exp(scores - highest)
    denominator = jnp.sum(expo, axis=-1, keepdims=True)
    probs = (expo / denominator).astype(jnp.bfloat16)
    attended = jnp.einsum(
        "rkgs,rksd->rkgd", probs, stored_values, preferred_element_type=jnp.float32
    )
    return attended.astype(jnp.bfloat16).reshape(row_count, QUERY_HEADS * HEAD_SIZE)


def spread(block, axis, count, groups=None):
    copies = jnp.broadcast_to(block[None], (count,) + block.shape)
    return lax.all_to_all(copies, axis, 0, 0, axis_index_groups=groups)


def swap(block, axis, count, bit):
    return lax.ppermute(block, axis, [(i, i ^ bit) for i in range(count)])


def gather_along_z(adapter_down, adapter_up):
    both = jnp.concatenate([adapter_down, adapter_up], axis=1)
    rank, width = both.shape
    return spread(both, "replica", DEPTH, Z_GROUPS).reshape(DEPTH * rank, width)


def gather_rest(some, split):
    for bit in (2, 1):
        other = swap(some, "replica", N_REPLICA, bit)
        some = jnp.concatenate([some, other], axis=0)
    return some[:, :split], some[:, split:]


def per_device(
    queries, stored_keys, stored_values, lengths, hidden, output_weight, adapter_down, adapter_up
):
    rows, width = hidden.shape
    some = gather_along_z(adapter_down, adapter_up)
    attended = attend_rows(queries, stored_keys, stored_values, lengths)
    blocks = attended.reshape(rows, 2, HALF, -1).transpose(2, 1, 0, 3)
    blocks = blocks.reshape(N_TENSOR, rows, -1)
    some, blocks = lax.optimization_barrier((some, blocks))
    down, up = gather_rest(some, adapter_down.shape[1])
    grouped = lax.all_to_all(blocks, "tensor", 0, 0, axis_index_groups=PLACE_GROUPS)
    grouped = grouped.reshape(N_TENSOR * rows, -1)
    hidden, grouped = lax.optimization_barrier((hidden, grouped))

    low_part = lax.dot_general(
        down, grouped, (((1,), (1,)), ((), ())), preferred_element_type=jnp.float32
    ).astype(jnp.bfloat16)
    by_rank = jnp.concatenate([low_part, up], axis=1)
    by_rank = lax.all_to_all(by_rank.reshape(N_TENSOR, -1, by_rank.shape[1]), "tensor", 0, 0)
    partial_value = jnp.dot(grouped, output_weight, preferred_element_type=jnp.float32)
    residual, upper, by_rank = lax.optimization_barrier(
        (hidden.astype(jnp.float32), lax.axis_index("tensor") >= HALF, by_rank)
    )
    low = jnp.sum(by_rank[:, :, : N_TENSOR * rows].astype(jnp.float32), axis=0)
    up = by_rank[:, :, N_TENSOR * rows :].transpose(1, 0, 2).reshape(-1, width)
    delta = lax.dot_general(
        low.astype(jnp.bfloat16), up, (((0,), (0,)), ((), ())), preferred_element_type=jnp.float32
    )
    partial_value = (partial_value + adapter_scale * delta).astype(jnp.bfloat16)
    received = lax.all_to_all(
        partial_value.reshape(HALF, 2 * rows, width),
        "tensor",
        0,
        0,
        axis_index_groups=HALF_GROUPS,
    )
    reduced = jnp.sum(received.astype(jnp.float32), axis=0)
    kept = jnp.where(upper, reduced[rows:], reduced[:rows])
    sent = jnp.where(upper, reduced[:rows], reduced[rows:]).astype(jnp.bfloat16)
    other = swap(sent, "tensor", N_TENSOR, HALF)
    return (residual + kept + other.astype(jnp.float32)).astype(jnp.bfloat16)


def solution(mesh):
    in_specs = (
        P(("replica", "tensor"), None),
        P(("replica", "tensor"), None, None, None),
        P(("replica", "tensor"), None, None, None),
        P(("replica", "tensor")),
        P(("replica", "tensor"), None),
        P("tensor", None),
        P("replica", "tensor"),
        P("replica", "tensor"),
    )
    out_specs = P(("replica", "tensor"), None)
    return jax.shard_map(
        per_device, mesh=mesh, in_specs=in_specs, out_specs=out_specs, check_vma=False
    )
```

```python
import math

import jax
import jax.numpy as jnp
from jax import lax
from jax.sharding import PartitionSpec as P

QUERY_HEADS = 64
KVH = 8
HEAD_SIZE = 128
CACHE = 128
GROUP = 8
N_TENSOR = 16
N_REPLICA = 64

adapter_scale = 2.0

HALF = 8
PLACE_GROUPS = [[half * HALF + near for near in range(HALF) for half in range(2)]]
HALF_GROUPS = [[upper * HALF + near for near in range(HALF)] for upper in range(2)]
DEPTH = 16
Z_GROUPS = [[z * 4 + rest for z in range(DEPTH)] for rest in range(4)]


def attend_rows(queries, stored_keys, stored_values, lengths):
    row_count = queries.shape[0]
    shaped = queries.reshape(row_count, KVH, GROUP, HEAD_SIZE)
    scores = jnp.einsum(
        "rkgd,rksd->rkgs", shaped, stored_keys, preferred_element_type=jnp.float32
    ) / math.sqrt(HEAD_SIZE)
    positions = jnp.arange(CACHE, dtype=jnp.int32)
    visible = positions[None, :] < lengths[:, None]
    scores = jnp.where(visible[:, None, None, :], scores, -1e30)
    highest = jnp.max(scores, axis=-1, keepdims=True)
    expo = jnp.exp(scores - highest)
    denominator = jnp.sum(expo, axis=-1, keepdims=True)
    probs = (expo / denominator).astype(jnp.bfloat16)
    attended = jnp.einsum(
        "rkgs,rksd->rkgd", probs, stored_values, preferred_element_type=jnp.float32
    )
    return attended.astype(jnp.bfloat16).reshape(row_count, QUERY_HEADS * HEAD_SIZE)


def spread(block, axis, count, groups=None):
    copies = jnp.broadcast_to(block[None], (count,) + block.shape)
    return lax.all_to_all(copies, axis, 0, 0, axis_index_groups=groups)


def swap(block, axis, count, bit):
    return lax.ppermute(block, axis, [(i, i ^ bit) for i in range(count)])


def gather_along_z(adapter_down, adapter_up):
    both = jnp.concatenate([adapter_down, adapter_up], axis=1)
    rank, width = both.shape
    return spread(both, "replica", DEPTH, Z_GROUPS).reshape(DEPTH * rank, width)


def gather_rest(some, split):
    for bit in (2, 1):
        other = swap(some, "replica", N_REPLICA, bit)
        some = jnp.concatenate([some, other], axis=0)
    return some[:, :split], some[:, split:]


def per_device(
    queries, stored_keys, stored_values, lengths, hidden, output_weight, adapter_down, adapter_up
):
    rows, width = hidden.shape
    some = gather_along_z(adapter_down, adapter_up)
    attended = attend_rows(queries, stored_keys, stored_values, lengths)
    blocks = attended.reshape(rows, 2, HALF, -1).transpose(2, 1, 0, 3)
    blocks = blocks.reshape(N_TENSOR, rows, -1)
    some, blocks = lax.optimization_barrier((some, blocks))
    down, up = gather_rest(some, adapter_down.shape[1])
    grouped = lax.all_to_all(blocks, "tensor", 0, 0, axis_index_groups=PLACE_GROUPS)
    grouped = grouped.reshape(N_TENSOR * rows, -1)

    low_part = lax.dot_general(
        down, grouped, (((1,), (1,)), ((), ())), preferred_element_type=jnp.float32
    ).astype(jnp.bfloat16)
    by_rank = jnp.concatenate([up, low_part], axis=1)
    split = up.shape[1]
    by_rank = lax.all_to_all(by_rank.reshape(N_TENSOR, -1, by_rank.shape[1]), "tensor", 0, 0)
    partial_value = jnp.dot(grouped, output_weight, preferred_element_type=jnp.float32)
    residual, upper, by_rank = lax.optimization_barrier(
        (hidden.astype(jnp.float32), lax.axis_index("tensor") >= HALF, by_rank)
    )
    low = jnp.sum(by_rank[:, :, split:].astype(jnp.float32), axis=0)
    up = by_rank[:, :, :split].transpose(1, 0, 2).reshape(-1, width)
    delta = lax.dot_general(
        low.astype(jnp.bfloat16), up, (((0,), (0,)), ((), ())), preferred_element_type=jnp.float32
    )
    partial_value = (partial_value + adapter_scale * delta).astype(jnp.bfloat16)
    received = lax.all_to_all(
        partial_value.reshape(HALF, 2 * rows, width),
        "tensor",
        0,
        0,
        axis_index_groups=HALF_GROUPS,
    )
    reduced = jnp.sum(received.astype(jnp.float32), axis=0)
    kept = jnp.where(upper, reduced[rows:], reduced[:rows])
    sent = jnp.where(upper, reduced[:rows], reduced[rows:]).astype(jnp.bfloat16)
    other = swap(sent, "tensor", N_TENSOR, HALF)
    return (residual + kept + other.astype(jnp.float32)).astype(jnp.bfloat16)


def solution(mesh):
    in_specs = (
        P(("replica", "tensor"), None),
        P(("replica", "tensor"), None, None, None),
        P(("replica", "tensor"), None, None, None),
        P(("replica", "tensor")),
        P(("replica", "tensor"), None),
        P("tensor", None),
        P("replica", "tensor"),
        P("replica", "tensor"),
    )
    out_specs = P(("replica", "tensor"), None)
    return jax.shard_map(
        per_device, mesh=mesh, in_specs=in_specs, out_specs=out_specs, check_vma=False
    )
```
